256 devices in a mesh: section: 64 (over z_lo, x, y, core), tensor: 4 (over z_hi).
Axes of the slice: x: 4, y: 4, z: 8 (z_hi: 4, z_lo: 2; z = z_hi * 2 + z_lo), core: 2. Of those that a mesh axis runs over, the one named last changes fastest.
Arguments:
- key_weight: bfloat16 [64, 4096, 512], P('section', None, 'tensor'), may hold values from -0.046875 to 0.046875
- first_moment: float32 [64, 4096, 512], P('section', None, 'tensor'), may hold values from -3 to 3
- second_moment: float32 [64, 4096, 512], P('section', None, 'tensor'), may hold values from 0.05 to 2
- down_inputs: bfloat16 [64, 256, 4096], P('section', None, 'tensor'), may hold values from -0.59765625 to 0.59765625
- up_inputs: bfloat16 [64, 256, 4096], P('section', None, 'tensor'), may hold values from -0.59765625 to 0.59765625
- down_key_grads: bfloat16 [64, 256, 512], P('section', None, 'tensor'), may hold values from -6 to 6
- up_key_grads: bfloat16 [64, 256, 512], P('section', None, 'tensor'), may hold values from -6 to 6
Outputs:
- new_weight: float32 [64, 4096, 512], P('section', None, 'tensor')
- new_first: float32 [64, 4096, 512], P('section', None, 'tensor')
- new_second: float32 [64, 4096, 512], P('section', None, 'tensor')
- down_received: bfloat16 [64, 4096, 256], P('section', 'tensor')
- up_received: bfloat16 [64, 4096, 256], P('section', 'tensor')
The draws below stay inside these ranges and needn't reach their ends.
All inputs are finite; a program needn't handle non-finite values.
Results may differ from the reference program's by a relative error of at most 0.006.
Values may be sent and summed in bfloat16 or wider, within the bound.
A program may use at most 128 MiB of HBM per device.

```python
import math
import jax
import jax.numpy as jnp
from jax import lax

D = 4096
TOK = 256
ADAM_STEP = 100
KVC = 512
SECTIONS = 64


def steps_of(key, shape, cuts, smallest, top_value):
    level = 1.0
    for axis_at, shards_of in cuts:
        draws = jax.random.uniform(jax.random.fold_in(jax.random.fold_in(key, 6), axis_at), (shards_of,), jnp.float32, smallest / len(cuts), top_value / len(cuts))
        level = level * jnp.repeat(jnp.exp(draws), shape[axis_at] // shards_of).reshape((-1,) + (1,) * (len(shape) - 1 - axis_at))
    return level


def bell_draw(stream_key, shape, spread, limit, cuts=(), held_as=jnp.bfloat16):
    values = spread * jax.random.normal(stream_key, shape, jnp.float32)
    if cuts:
        values = values * steps_of(stream_key, shape, cuts, -0.22, 0.18)
    return jnp.clip(values, -limit, limit).astype(held_as)


def setup_inputs(seed: int = 0) -> dict:
    seeds = jax.random.split(jax.random.key(seed), 8)
    return {
        "key_weight": bell_draw(seeds[0], (SECTIONS, D, KVC), (4 * D) ** -0.5, 0.046875, ((0, 64), (2, 4))),
        "first_moment": bell_draw(seeds[1], (SECTIONS, D, KVC), 0.5, 3.0, ((0, 64), (2, 4)), jnp.float32),
        "second_moment": jnp.clip(jnp.exp(math.log(2.0) - 3.6888794 * jax.random.uniform(seeds[2], (SECTIONS, D, KVC), jnp.float32) ** steps_of(seeds[2], (SECTIONS, D, KVC), ((0, 64), (2, 4)), -0.2, 0.2)), 0.05, 2.0),
        "down_inputs": bell_draw(seeds[3], (SECTIONS, TOK, D), 0.1, 0.59765625, ((0, 64), (2, 4))),
        "up_inputs": bell_draw(seeds[4], (SECTIONS, TOK, D), 0.1, 0.59765625, ((0, 64), (2, 4))),
        "down_key_grads": bell_draw(seeds[5], (SECTIONS, TOK, KVC), 1.0, 6.0, ((0, 64), (2, 4))),
        "up_key_grads": bell_draw(seeds[6], (SECTIONS, TOK, KVC), 1.0, 6.0, ((0, 64), (2, 4))),
    }


beta_one = 0.9
beta_two = 0.95
learn_rate = 0.00015
decay_rate = 0.1
epsilon = 1e-08

def block_grad(operands):
    return jnp.einsum('td,tc->dc', operands[0].astype(jnp.float32), operands[1].astype(jnp.float32))

def block_term(operands):
    return jnp.dot(operands[0], operands[1].T, preferred_element_type=jnp.float32).astype(jnp.bfloat16)

def reference(key_weight, first_moment, second_moment, down_inputs, up_inputs, down_key_grads, up_key_grads):
    down_grad = lax.map(block_grad, (down_inputs, down_key_grads))
    up_grad = lax.map(block_grad, (up_inputs, up_key_grads))
    gradient = down_grad + jnp.flip(up_grad, 0)
    new_first = beta_one * first_moment + (1.0 - beta_one) * gradient
    new_second = beta_two * second_moment + (1.0 - beta_two) * gradient * gradient
    first_hat = new_first / (1.0 - beta_one ** ADAM_STEP)
    second_hat = new_second / (1.0 - beta_two ** ADAM_STEP)
    weight_full = key_weight.astype(jnp.float32)
    new_weight = weight_full - learn_rate * (first_hat / (jnp.sqrt(second_hat) + epsilon) + decay_rate * weight_full)
    down_term = lax.map(block_term, (key_weight, down_key_grads))
    up_term = lax.map(block_term, (jnp.flip(key_weight, 0), up_key_grads))
    zero_block = jnp.zeros_like(down_term[:1])
    down_received = jnp.concatenate([down_term[1:], zero_block], 0)
    up_received = jnp.concatenate([zero_block, up_term[:-1]], 0)
    return (new_weight, new_first, new_second, down_received, up_received)
```

```python
import jax
import jax.numpy as jnp
from jax import lax
from jax.experimental import pallas as pl
from jax.experimental.pallas import tpu as pltpu
from jax.sharding import PartitionSpec as P

ADAM_STEP = 100


beta_one = 0.9
beta_two = 0.95
learn_rate = 0.00015
decay_rate = 0.1
epsilon = 1e-08

MESH = pl.DeviceIdType.MESH
CHUNKS = 4


def relay_kernel(
    sections,
    ways,
    weight,
    down_rows,
    up_rows,
    down_grads,
    up_grads,
    grad_out,
    down_out,
    up_out,
    tokens,
    keys,
    rows,
    grads,
    down_term,
    up_term,
    local_sem,
    key_send,
    key_recv,
    mirror_key_send,
    mirror_key_recv,
    row_send,
    row_recv,
    weight_send,
    weight_recv,
    grad_send,
    grad_recv,
    term_send,
    term_recv,
):
    s = lax.axis_index("section")
    t = lax.axis_index("tensor")
    mirror = sections - 1 - s
    after = sections - s
    toks = down_rows.shape[0]
    feats = down_rows.shape[1]
    cols = down_grads.shape[1]
    step = feats // CHUNKS
    others = range(1, ways)
    along = [lax.rem(t + d, ways) for d in range(ways)]

    def remote(src, dst, send, recv, where):
        return pltpu.make_async_remote_copy(
            src_ref=src, dst_ref=dst, send_sem=send, recv_sem=recv, device_id=where, device_id_type=MESH
        )

    own = [
        pltpu.make_async_copy(down_grads, keys.at[0, pl.ds(0, toks)], local_sem.at[0]),
        pltpu.make_async_copy(down_rows, tokens.at[pl.ds(0, toks)], local_sem.at[1]),
        pltpu.make_async_copy(weight.at[pl.ds(t * feats, feats)], rows.at[0], local_sem.at[2]),
    ]
    for copy in own:
        copy.start()

    barrier = pltpu.get_barrier_semaphore()

    def greet(where):
        pl.semaphore_signal(barrier, inc=1, device_id=where, device_id_type=MESH)

    for d in others:
        greet((s, along[d]))
    for d in range(ways):
        greet((mirror, along[d]))

    @pl.when(s < sections - 1)
    def _():
        greet((s + 1, t))

    has_next = s > 0
    is_own = after == s

    swaps = jnp.logical_and(has_next, jnp.logical_not(is_own))

    @pl.when(swaps)
    def _():
        greet((after, t))

    sent_to = 2 * ways - 1 + has_next.astype(jnp.int32) + swaps.astype(jnp.int32)
    pl.semaphore_wait(barrier, sent_to)

    mirror_key_copies = [
        remote(
            up_grads,
            keys.at[(ways - d) % ways, pl.ds(toks, toks)],
            mirror_key_send.at[d],
            mirror_key_recv.at[(ways - d) % ways],
            (mirror, along[d]),
        )
        for d in range(ways)
    ]
    key_copies = [
        remote(
            down_grads,
            keys.at[ways - d, pl.ds(0, toks)],
            key_send.at[d],
            key_recv.at[ways - d],
            (s, along[d]),
        )
        for d in others
    ]
    row_copies = [
        remote(
            up_rows.at[:, pl.ds(c * step, step)],
            tokens.at[pl.ds(toks, toks), pl.ds(c * step, step)],
            row_send.at[c],
            row_recv.at[c],
            (mirror, t),
        )
        for c in range(CHUNKS)
    ]
    weight_copies = [
        [
            remote(
                weight.at[pl.ds(along[d] * feats + c * step, step)],
                rows.at[ways - d, pl.ds(c * step, step)],
                weight_send.at[c, d],
                weight_recv.at[c, ways - d],
                (s, along[d]),
            )
            for d in others
        ]
        for c in range(CHUNKS)
    ]
    for copy in mirror_key_copies + key_copies + row_copies:
        copy.start()
    for copies in weight_copies:
        for copy in copies:
            copy.start()

    own[0].wait()
    own[1].wait()
    for copy in mirror_key_copies + key_copies:
        copy.wait_recv()
    grad_copies = []
    for c in range(CHUNKS):
        part = pl.ds(c * step, step)
        row_copies[c].wait_recv()
        all_keys = jnp.concatenate([keys[d] for d in range(ways)], axis=1)
        found = lax.dot_general(
            tokens[:, part], all_keys, (((0,), (0,)), ((), ())), preferred_element_type=jnp.float32
        ).astype(jnp.bfloat16)
        for d in range(ways):
            grads[d, part] = found[:, d * cols : (d + 1) * cols]
        for d in others:
            copy = remote(
                grads.at[d, part],
                grad_out.at[t, part],
                grad_send.at[c, d],
                grad_recv.at[c, ways - d],
                (s, along[d]),
            )
            copy.start()
            grad_copies.append(copy)
    own_grad = pltpu.make_async_copy(grads.at[0], grad_out.at[t], local_sem.at[3])
    own_grad.start()

    own[2].wait()

    def term_copies(c):
        part = pl.ds(c * step, step)
        down = remote(
            down_term.at[part], down_out.at[part], term_send.at[0, c], term_recv.at[0, c], (s - 1, t)
        )
        up = remote(
            up_term.at[part], up_out.at[part], term_send.at[1, c], term_recv.at[1, c], (after, t)
        )
        stay = pltpu.make_async_copy(up_term.at[part], up_out.at[part], term_send.at[1, c])
        return down, up, stay

    for c in range(CHUNKS):
        part = pl.ds(c * step, step)
        for copy in weight_copies[c]:
            copy.wait_recv()
        all_keys = jnp.concatenate([keys[d] for d in range(ways)], axis=1)
        all_rows = jnp.concatenate([rows[d, part] for d in range(ways)], axis=1)
        found = lax.dot_general(
            all_rows, all_keys, (((1,), (1,)), ((), ())), preferred_element_type=jnp.float32
        ).astype(jnp.bfloat16)
        down_term[part] = found[:, :toks]
        up_term[part] = found[:, toks:]
        down, up, stay = term_copies(c)

        @pl.when(has_next)
        def _():
            @pl.when(is_own)
            def _():
                stay.start()

            @pl.when(jnp.logical_not(is_own))
            def _():
                up.start()

            down.start()

    def clear(out, from_term):
        from_term[...] = jnp.zeros_like(from_term)
        fill = pltpu.make_async_copy(from_term, out, local_sem.at[4])
        fill.start()
        fill.wait()

    @pl.when(s == 0)
    def _():
        clear(up_out, up_term)

    for c in range(CHUNKS):
        down, up, stay = term_copies(c)

        @pl.when(s < sections - 1)
        def _():
            down.wait_recv()

        @pl.when(has_next)
        def _():
            @pl.when(is_own)
            def _():
                stay.wait()

            @pl.when(jnp.logical_not(is_own))
            def _():
                up.wait()

            down.wait_send()

    @pl.when(s == sections - 1)
    def _():
        clear(down_out, down_term)

    own_grad.wait()
    for copy in grad_copies:
        copy.wait()
    for copy in mirror_key_copies + key_copies + row_copies:
        copy.wait_send()
    for copies in weight_copies:
        for copy in copies:
            copy.wait_send()


def relay(sections, ways, weight, down_rows, up_rows, down_grads, up_grads):
    feats, toks, cols = down_rows.shape[1], down_rows.shape[0], down_grads.shape[1]
    dma = pltpu.SemaphoreType.DMA
    anywhere = pl.BlockSpec(memory_space=pl.ANY)
    return pl.pallas_call(
        lambda *refs: relay_kernel(sections, ways, *refs),
        out_shape=(
            jax.ShapeDtypeStruct((ways, feats, cols), jnp.bfloat16),
            jax.ShapeDtypeStruct((feats, toks), jnp.bfloat16),
            jax.ShapeDtypeStruct((feats, toks), jnp.bfloat16),
        ),
        in_specs=[anywhere] * 5,
        out_specs=(anywhere,) * 3,
        scratch_shapes=[
            pltpu.VMEM((2 * toks, feats), jnp.bfloat16),
            pltpu.VMEM((ways, 2 * toks, cols), jnp.bfloat16),
            pltpu.VMEM((ways, feats, cols), jnp.bfloat16),
            pltpu.VMEM((ways, feats, cols), jnp.bfloat16),
            pltpu.VMEM((feats, toks), jnp.bfloat16),
            pltpu.VMEM((feats, toks), jnp.bfloat16),
            dma((5,)),
            dma((ways,)),
            dma((ways,)),
            dma((ways,)),
            dma((ways,)),
            dma((CHUNKS,)),
            dma((CHUNKS,)),
            dma((CHUNKS, ways)),
            dma((CHUNKS, ways)),
            dma((CHUNKS, ways)),
            dma((CHUNKS, ways)),
            dma((2, CHUNKS)),
            dma((2, CHUNKS)),
        ],
        compiler_params=pltpu.CompilerParams(
            collective_id=0, has_side_effects=True, vmem_limit_bytes=60 * 1024 * 1024
        ),
    )(weight, down_rows, up_rows, down_grads, up_grads)


def local(
    key_weight, first_moment, second_moment, down_inputs, up_inputs, down_key_grads, up_key_grads
):
    weight = key_weight[0]
    gradient, down_received, up_received = relay(
        lax.axis_size("section"),
        lax.axis_size("tensor"),
        weight,
        down_inputs[0],
        up_inputs[0],
        down_key_grads[0],
        up_key_grads[0],
    )
    gradient = gradient.reshape(weight.shape).astype(jnp.float32)
    new_first = beta_one * first_moment[0] + (1.0 - beta_one) * gradient
    new_second = beta_two * second_moment[0] + (1.0 - beta_two) * gradient * gradient
    first_hat = new_first / (1.0 - beta_one**ADAM_STEP)
    second_hat = new_second / (1.0 - beta_two**ADAM_STEP)
    weight_full = weight.astype(jnp.float32)
    new_weight = weight_full - learn_rate * (
        first_hat / (jnp.sqrt(second_hat) + epsilon) + decay_rate * weight_full
    )
    return (
        new_weight[None],
        new_first[None],
        new_second[None],
        down_received[None],
        up_received[None],
    )


def solution(mesh):
    in_specs = (
        P("section", None, "tensor"),
        P("section", None, "tensor"),
        P("section", None, "tensor"),
        P("section", None, "tensor"),
        P("section", None, "tensor"),
        P("section", None, "tensor"),
        P("section", None, "tensor"),
    )
    out_specs = (
        P("section", None, "tensor"),
        P("section", None, "tensor"),
        P("section", None, "tensor"),
        P("section", "tensor", None),
        P("section", "tensor", None),
    )
    return jax.shard_map(local, mesh=mesh, in_specs=in_specs, out_specs=out_specs, check_vma=False)
```

```python
import jax
import jax.numpy as jnp
from jax import lax
from jax.experimental import pallas as pl
from jax.experimental.pallas import tpu as pltpu
from jax.sharding import PartitionSpec as P

ADAM_STEP = 100


beta_one = 0.9
beta_two = 0.95
learn_rate = 0.00015
decay_rate = 0.1
epsilon = 1e-08

MESH = pl.DeviceIdType.MESH
CHUNKS = 4


def relay_kernel(
    sections,
    ways,
    weight,
    first_moment,
    second_moment,
    down_rows,
    up_rows,
    down_grads,
    up_grads,
    weight_out,
    first_out,
    second_out,
    down_out,
    up_out,
    own_weight,
    own_first,
    own_second,
    tokens,
    keys,
    rows,
    grads,
    arrived,
    down_term,
    up_term,
    passing,
    local_sem,
    key_send,
    key_recv,
    row_send,
    row_recv,
    weight_send,
    weight_recv,
    grad_send,
    grad_recv,
    term_send,
    term_recv,
    pass_recv,
):
    s = lax.axis_index("section")
    t = lax.axis_index("tensor")
    mirror = sections - 1 - s
    after = sections - s
    half = sections // 2
    toks, feats = down_rows.shape
    cols = down_grads.shape[1]
    step = feats // CHUNKS
    others = range(1, ways)
    back = ways - 1
    far = ways // 2
    along = [lax.rem(t + d, ways) for d in range(ways)]
    down_part, up_part = pl.ds(0, toks), pl.ds(toks, toks)

    def remote(src, dst, send, recv, where):
        return pltpu.make_async_remote_copy(
            src_ref=src, dst_ref=dst, send_sem=send, recv_sem=recv, device_id=where, device_id_type=MESH
        )

    barrier = pltpu.get_barrier_semaphore()

    def greet(where):
        pl.semaphore_signal(barrier, inc=1, device_id=where, device_id_type=MESH)

    for d in others:
        greet((s, along[d]))
    greet((mirror, t))

    first, last, middle = s == 0, s == sections - 1, s == half
    joint = s == half - 1

    @pl.when(jnp.logical_not(jnp.logical_or(last, joint)))
    def _():
        greet((s + 1, t))

    @pl.when(joint)
    def _():
        greet((0, t))

    @pl.when(first)
    def _():
        greet((half, t))

    swaps = jnp.logical_not(jnp.logical_or(first, middle))

    @pl.when(swaps)
    def _():
        greet((after, t))

    own = [
        pltpu.make_async_copy(down_grads, keys.at[0, down_part], local_sem.at[0]),
        pltpu.make_async_copy(down_rows, tokens.at[down_part], local_sem.at[1]),
    ]
    for d in range(ways):
        block = pl.ds(along[d] * feats, feats)
        own += [
            pltpu.make_async_copy(weight.at[block], own_weight.at[d], local_sem.at[2 + 3 * d]),
            pltpu.make_async_copy(first_moment.at[block], own_first.at[d], local_sem.at[3 + 3 * d]),
            pltpu.make_async_copy(second_moment.at[block], own_second.at[d], local_sem.at[4 + 3 * d]),
        ]
    for copy in own:
        copy.start()

    pl.semaphore_wait(barrier, ways + 1 + swaps.astype(jnp.int32))

    to_mirror = remote(up_grads, keys.at[0, up_part], key_send.at[0], key_recv.at[0], (mirror, t))
    down_keys = {
        1: remote(down_grads, keys.at[back, down_part], key_send.at[1], key_recv.at[1], (s, along[1])),
        back: remote(down_grads, keys.at[1, down_part], key_send.at[2], key_recv.at[2], (s, along[back])),
    }
    up_keys = {
        1: remote(keys.at[0, up_part], keys.at[back, up_part], key_send.at[3], key_recv.at[3], (s, along[1])),
        back: remote(keys.at[0, up_part], keys.at[1, up_part], key_send.at[4], key_recv.at[4], (s, along[back])),
    }
    far_down = remote(
        keys.at[back, down_part], keys.at[far, down_part], key_send.at[5], key_recv.at[5], (s, along[1])
    )
    far_up = remote(
        keys.at[1, up_part], keys.at[far, up_part], key_send.at[6], key_recv.at[6], (s, along[back])
    )
    row_copies = [
        remote(
            up_rows.at[:, pl.ds(c * step, step)],
            tokens.at[up_part, pl.ds(c * step, step)],
            row_send.at[c],
            row_recv.at[c],
            (mirror, t),
        )
        for c in range(CHUNKS)
    ]
    weight_copies = [
        [
            remote(
                weight.at[pl.ds(along[d] * feats + c * step, step)],
                rows.at[ways - d, pl.ds(c * step, step)],
                weight_send.at[c, d],
                weight_recv.at[c, ways - d],
                (s, along[d]),
            )
            for d in others
        ]
        for c in range(CHUNKS)
    ]
    to_mirror.start()
    down_keys[1].start()
    down_keys[back].start()
    for copy in weight_copies[0]:
        copy.start()
    to_mirror.wait_recv()
    up_keys[1].start()
    up_keys[back].start()
    down_keys[1].wait_recv()
    far_down.start()
    up_keys[back].wait_recv()
    far_up.start()
    for copies in weight_copies[1:]:
        for copy in copies:
            copy.start()
    for copy in row_copies:
        copy.start()
    for copy in own:
        copy.wait()
    for copy in (down_keys[back], up_keys[1], far_down, far_up):
        copy.wait_recv()

    def down_copy(c):
        part = pl.ds(c * step, step)
        return remote(
            down_term.at[part], down_out.at[part], term_send.at[0, c], term_recv.at[0, c], (s - 1, t)
        )

    def first_leg(c):
        part = pl.ds(c * step, step)
        return remote(down_term.at[part], passing.at[part], term_send.at[0, c], pass_recv.at[c], (0, t))

    def second_leg(c):
        part = pl.ds(c * step, step)
        return remote(
            passing.at[part], down_out.at[part], term_send.at[0, c], term_recv.at[0, c], (half - 1, t)
        )

    def up_copy(c):
        part = pl.ds(c * step, step)
        return remote(
            up_term.at[part], up_out.at[part], term_send.at[1, c], term_recv.at[1, c], (after, t)
        )

    sends_on = jnp.logical_not(jnp.logical_or(first, middle))

    for c in range(CHUNKS):
        part = pl.ds(c * step, step)
        for copy in weight_copies[c]:
            copy.wait_recv()
        all_keys = jnp.concatenate([keys[d] for d in range(ways)], axis=1)
        all_rows = jnp.concatenate(
            [own_weight[0, part]] + [rows[d, part] for d in others], axis=1
        )
        found = lax.dot_general(
            all_rows, all_keys, (((1,), (1,)), ((), ())), preferred_element_type=jnp.float32
        ).astype(jnp.bfloat16)
        down_term[part] = found[:, :toks]
        up_term[part] = found[:, toks:]

        @pl.when(sends_on)
        def _():
            up_copy(c).start()
            down_copy(c).start()

        @pl.when(middle)
        def _():
            first_leg(c).start()
            up_out[part] = found[:, toks:]

    def grad_copies(c):
        part = pl.ds(c * step, step)
        return [
            remote(
                grads.at[d, part],
                arrived.at[ways - d, part],
                grad_send.at[c, d],
                grad_recv.at[c, ways - d],
                (s, along[d]),
            )
            for d in others
        ]

    for c in range(CHUNKS):
        part = pl.ds(c * step, step)
        row_copies[c].wait_recv()
        all_keys = jnp.concatenate([keys[d] for d in range(ways)], axis=1)
        found = lax.dot_general(
            tokens[:, part], all_keys, (((0,), (0,)), ((), ())), preferred_element_type=jnp.float32
        ).astype(jnp.bfloat16)
        for d in range(ways):
            grads[d, part] = found[:, d * cols : (d + 1) * cols]
        for copy in grad_copies(c):
            copy.start()

    @pl.when(first)
    def _():
        for c in range(CHUNKS):
            first_leg(c).wait_recv()
            second_leg(c).start()

    @pl.when(first)
    def _():
        up_out[...] = jnp.zeros_like(up_out)

    @pl.when(last)
    def _():
        down_out[...] = jnp.zeros_like(down_out)

    def update(d, c, gradient):
        part = pl.ds(c * step, step)
        here = pl.ds(pl.multiple_of(along[d] * feats + c * step, step), step)
        gradient = gradient.astype(jnp.float32)
        new_first = beta_one * own_first[d, part] + (1.0 - beta_one) * gradient
        new_second = beta_two * own_second[d, part] + (1.0 - beta_two) * gradient * gradient
        first_hat = new_first * (1.0 / (1.0 - beta_one**ADAM_STEP))
        second_hat = new_second * (1.0 / (1.0 - beta_two**ADAM_STEP))
        held = own_weight[d, part].astype(jnp.float32)
        first_out[here] = new_first
        second_out[here] = new_second
        weight_out[here] = held - learn_rate * (
            first_hat / (jnp.sqrt(second_hat) + epsilon) + decay_rate * held
        )

    for c in range(CHUNKS):
        update(0, c, grads[0, pl.ds(c * step, step)])

    for c in range(CHUNKS):
        for copy, d in zip(grad_copies(c), others):
            copy.wait_recv()
            update(ways - d, c, arrived[ways - d, pl.ds(c * step, step)])

    for c in range(CHUNKS):
        @pl.when(jnp.logical_not(last))
        def _():
            down_copy(c).wait_recv()

        @pl.when(swaps)
        def _():
            up_copy(c).wait_recv()

    for c in range(CHUNKS):
        for copy in grad_copies(c) + weight_copies[c]:
            copy.wait_send()

        down_copy(c).wait_send()

        @pl.when(swaps)
        def _():
            up_copy(c).wait_send()

    for copy in [to_mirror, *down_keys.values(), *up_keys.values(), far_down, far_up, *row_copies]:
        copy.wait_send()


def relay(sections, ways, weight, first_moment, second_moment, down_rows, up_rows, down_grads, up_grads):
    feats, toks, cols = down_rows.shape[1], down_rows.shape[0], down_grads.shape[1]
    dma = pltpu.SemaphoreType.DMA
    state = pltpu.VMEM(weight.shape, jnp.float32)
    term = pltpu.VMEM((feats, toks), jnp.bfloat16)
    block = (ways, feats, cols)
    operands = [
        pltpu.with_memory_space_constraint(x, pltpu.HBM)
        for x in (weight, first_moment, second_moment, down_rows, up_rows, down_grads, up_grads)
    ]
    return pl.pallas_call(
        lambda *refs: relay_kernel(sections, ways, *refs),
        out_shape=(state, state, state, term, term),
        in_specs=[pl.BlockSpec(memory_space=pltpu.HBM)] * 7,
        out_specs=(pl.BlockSpec(memory_space=pltpu.VMEM),) * 5,
        scratch_shapes=[
            pltpu.VMEM(block, jnp.bfloat16),
            pltpu.VMEM(block, jnp.float32),
            pltpu.VMEM(block, jnp.float32),
            pltpu.VMEM((2 * toks, feats), jnp.bfloat16),
            pltpu.VMEM((ways, 2 * toks, cols), jnp.bfloat16),
            pltpu.VMEM(block, jnp.bfloat16),
            pltpu.VMEM(block, jnp.bfloat16),
            pltpu.VMEM(block, jnp.bfloat16),
            pltpu.VMEM((feats, toks), jnp.bfloat16),
            pltpu.VMEM((feats, toks), jnp.bfloat16),
            pltpu.VMEM((feats, toks), jnp.bfloat16),
            dma((2 + 3 * ways,)),
            dma((7,)),
            dma((7,)),
            dma((CHUNKS,)),
            dma((CHUNKS,)),
            dma((CHUNKS, ways)),
            dma((CHUNKS, ways)),
            dma((CHUNKS, ways)),
            dma((CHUNKS, ways)),
            dma((2, CHUNKS)),
            dma((2, CHUNKS)),
            dma((CHUNKS,)),
        ],
        compiler_params=pltpu.CompilerParams(
            collective_id=0, has_side_effects=True, vmem_limit_bytes=16 * 1024 * 1024
        ),
    )(*operands)


def leave_kernel(*refs):
    count = len(refs) // 2
    sems = refs[-1]
    copies = [
        pltpu.make_async_copy(refs[i], refs[count + i], sems.at[i]) for i in range(count)
    ]
    for copy in copies:
        copy.start()
    for copy in copies:
        copy.wait()


def leave(*arrays):
    return pl.pallas_call(
        leave_kernel,
        out_shape=tuple(jax.ShapeDtypeStruct(x.shape, x.dtype) for x in arrays),
        in_specs=[pl.BlockSpec(memory_space=pltpu.VMEM)] * len(arrays),
        out_specs=(pl.BlockSpec(memory_space=pl.ANY),) * len(arrays),
        scratch_shapes=[pltpu.SemaphoreType.DMA((len(arrays),))],
        compiler_params=pltpu.CompilerParams(vmem_limit_bytes=16 * 1024 * 1024),
    )(*(pltpu.with_memory_space_constraint(x, pltpu.VMEM) for x in arrays))


def local(
    key_weight, first_moment, second_moment, down_inputs, up_inputs, down_key_grads, up_key_grads
):
    arrays = relay(
        lax.axis_size("section"),
        lax.axis_size("tensor"),
        key_weight[0],
        first_moment[0],
        second_moment[0],
        down_inputs[0],
        up_inputs[0],
        down_key_grads[0],
        up_key_grads[0],
    )
    return tuple(x[None] for x in leave(*arrays))


def solution(mesh):
    in_specs = (
        P("section", None, "tensor"),
        P("section", None, "tensor"),
        P("section", None, "tensor"),
        P("section", None, "tensor"),
        P("section", None, "tensor"),
        P("section", None, "tensor"),
        P("section", None, "tensor"),
    )
    out_specs = (
        P("section", None, "tensor"),
        P("section", None, "tensor"),
        P("section", None, "tensor"),
        P("section", "tensor", None),
        P("section", "tensor", None),
    )
    return jax.shard_map(local, mesh=mesh, in_specs=in_specs, out_specs=out_specs, check_vma=False)
```

```python
import jax
import jax.numpy as jnp
from jax import lax
from jax.experimental import pallas as pl
from jax.experimental.pallas import tpu as pltpu
from jax.sharding import PartitionSpec as P

ADAM_STEP = 100


beta_one = 0.9
beta_two = 0.95
learn_rate = 0.00015
decay_rate = 0.1
epsilon = 1e-08

MESH = pl.DeviceIdType.MESH
CHUNKS = 4


def relay_kernel(
    sections,
    ways,
    weight,
    first_moment,
    second_moment,
    down_rows,
    up_rows,
    down_grads,
    up_grads,
    weight_out,
    first_out,
    second_out,
    down_out,
    up_out,
    own_weight,
    own_first,
    own_second,
    tokens,
    keys,
    rows,
    grads,
    arrived,
    down_term,
    up_term,
    passing,
    local_sem,
    key_send,
    key_recv,
    row_send,
    row_recv,
    weight_send,
    weight_recv,
    grad_send,
    grad_recv,
    term_send,
    term_recv,
    pass_recv,
):
    s = lax.axis_index("section")
    t = lax.axis_index("tensor")
    mirror = sections - 1 - s
    after = sections - s
    half = sections // 2
    toks, feats = down_rows.shape
    cols = down_grads.shape[1]
    step = feats // CHUNKS
    others = range(1, ways)
    back = ways - 1
    far = ways // 2
    along = [lax.rem(t + d, ways) for d in range(ways)]
    down_part, up_part = pl.ds(0, toks), pl.ds(toks, toks)

    def remote(src, dst, send, recv, where):
        return pltpu.make_async_remote_copy(
            src_ref=src, dst_ref=dst, send_sem=send, recv_sem=recv, device_id=where, device_id_type=MESH
        )

    barrier = pltpu.get_barrier_semaphore()

    def greet(where):
        pl.semaphore_signal(barrier, inc=1, device_id=where, device_id_type=MESH)

    for d in others:
        greet((s, along[d]))
    greet((mirror, t))
    greet((mirror, lax.rem(t + jnp.where(s < half, back, 1), ways)))

    first, last, middle = s == 0, s == sections - 1, s == half
    joint = s == half - 1

    @pl.when(jnp.logical_not(jnp.logical_or(last, joint)))
    def _():
        greet((s + 1, t))

    @pl.when(joint)
    def _():
        greet((0, t))

    @pl.when(first)
    def _():
        greet((half, t))

    swaps = jnp.logical_not(jnp.logical_or(first, middle))

    @pl.when(swaps)
    def _():
        greet((after, t))

    own = [
        pltpu.make_async_copy(down_grads, keys.at[0, down_part], local_sem.at[0]),
        pltpu.make_async_copy(down_rows, tokens.at[down_part], local_sem.at[1]),
    ]
    for d in range(ways):
        block = pl.ds(along[d] * feats, feats)
        own += [
            pltpu.make_async_copy(weight.at[block], own_weight.at[d], local_sem.at[2 + 3 * d]),
            pltpu.make_async_copy(first_moment.at[block], own_first.at[d], local_sem.at[3 + 3 * d]),
            pltpu.make_async_copy(second_moment.at[block], own_second.at[d], local_sem.at[4 + 3 * d]),
        ]
    for copy in own:
        copy.start()

    pl.semaphore_wait(barrier, ways + 2 + swaps.astype(jnp.int32))

    turn = jnp.where(s < half, 1, back)
    other = ways - turn
    ahead, behind = (s, lax.rem(t + turn, ways)), (s, lax.rem(t + other, ways))
    to_mirror = remote(up_grads, keys.at[0, up_part], key_send.at[0], key_recv.at[0], (mirror, t))
    to_side = remote(
        up_grads, keys.at[turn, up_part], key_send.at[1], key_recv.at[1], (mirror, lax.rem(t + other, ways))
    )
    down_ahead = remote(down_grads, keys.at[other, down_part], key_send.at[2], key_recv.at[2], ahead)
    down_behind = remote(down_grads, keys.at[turn, down_part], key_send.at[3], key_recv.at[3], behind)
    up_behind = remote(keys.at[0, up_part], keys.at[turn, up_part], key_send.at[4], key_recv.at[4], behind)
    both_far = remote(keys.at[other], keys.at[far], key_send.at[5], key_recv.at[5], ahead)
    row_copies = [
        remote(
            up_rows.at[:, pl.ds(c * step, step)],
            tokens.at[up_part, pl.ds(c * step, step)],
            row_send.at[c],
            row_recv.at[c],
            (mirror, t),
        )
        for c in range(CHUNKS)
    ]
    weight_copies = [
        [
            remote(
                weight.at[pl.ds(along[d] * feats + c * step, step)],
                rows.at[ways - d, pl.ds(c * step, step)],
                weight_send.at[c, d],
                weight_recv.at[c, ways - d],
                (s, along[d]),
            )
            for d in others
        ]
        for c in range(CHUNKS)
    ]
    for copy in (to_mirror, to_side, down_ahead, down_behind):
        copy.start()
    for copy in weight_copies[0]:
        copy.start()
    to_mirror.wait_recv()
    up_behind.start()
    to_side.wait_recv()
    down_ahead.wait_recv()
    both_far.start()
    for copies in weight_copies[1:]:
        for copy in copies:
            copy.start()
    for copy in row_copies:
        copy.start()
    for copy in own:
        copy.wait()
    for copy in (down_behind, up_behind, both_far):
        copy.wait_recv()

    def down_copy(c):
        part = pl.ds(c * step, step)
        return remote(
            down_term.at[part], down_out.at[part], term_send.at[0, c], term_recv.at[0, c], (s - 1, t)
        )

    def first_leg(c):
        part = pl.ds(c * step, step)
        return remote(down_term.at[part], passing.at[part], term_send.at[0, c], pass_recv.at[c], (0, t))

    def second_leg(c):
        part = pl.ds(c * step, step)
        return remote(
            passing.at[part], down_out.at[part], term_send.at[0, c], term_recv.at[0, c], (half - 1, t)
        )

    def up_copy(c):
        part = pl.ds(c * step, step)
        return remote(
            up_term.at[part], up_out.at[part], term_send.at[1, c], term_recv.at[1, c], (after, t)
        )

    sends_on = jnp.logical_not(jnp.logical_or(first, middle))

    def make_terms(c):
        part = pl.ds(c * step, step)
        for copy in weight_copies[c]:
            copy.wait_recv()
        all_keys = jnp.concatenate([keys[d] for d in range(ways)], axis=1)
        all_rows = jnp.concatenate(
            [own_weight[0, part]] + [rows[d, part] for d in others], axis=1
        )
        found = lax.dot_general(
            all_rows, all_keys, (((1,), (1,)), ((), ())), preferred_element_type=jnp.float32
        ).astype(jnp.bfloat16)
        down_term[part] = found[:, :toks]
        up_term[part] = found[:, toks:]

        @pl.when(sends_on)
        def _():
            up_copy(c).start()

        @pl.when(middle)
        def _():
            first_leg(c).start()
            up_out[part] = found[:, toks:]


    def grad_copies(c):
        part = pl.ds(c * step, step)
        return [
            remote(
                grads.at[d, part],
                arrived.at[ways - d, part],
                grad_send.at[c, d],
                grad_recv.at[c, ways - d],
                (s, along[d]),
            )
            for d in others
        ]

    def send_grads(c, low, high):
        part = pl.ds(c * step, step)
        for there in range(low, high):
            d = lax.rem(there + ways - t, ways)

            @pl.when(d != 0)
            def _():
                remote(
                    grads.at[d, part],
                    arrived.at[ways - d, part],
                    grad_send.at[c, d],
                    grad_recv.at[c, ways - d],
                    (s, there),
                ).start()

    def make_grads(c):
        part = pl.ds(c * step, step)
        row_copies[c].wait_recv()
        all_keys = jnp.concatenate([keys[d] for d in range(ways)], axis=1)
        found = lax.dot_general(
            tokens[:, part], all_keys, (((0,), (0,)), ((), ())), preferred_element_type=jnp.float32
        ).astype(jnp.bfloat16)
        for d in range(ways):
            grads[d, part] = found[:, d * cols : (d + 1) * cols]

    make_terms(0)
    make_terms(1)
    make_grads(0)
    send_grads(0, 0, far)
    make_terms(2)
    make_grads(1)
    send_grads(1, 0, far)
    send_grads(0, far, ways)
    make_terms(3)
    make_grads(2)
    send_grads(2, 0, far)
    send_grads(1, far, ways)
    make_grads(3)
    send_grads(3, 0, far)
    send_grads(2, far, ways)
    send_grads(3, far, ways)

    @pl.when(sends_on)
    def _():
        for c in range(CHUNKS):
            down_copy(c).start()

    @pl.when(first)
    def _():
        for c in range(CHUNKS):
            first_leg(c).wait_recv()
            second_leg(c).start()

    @pl.when(first)
    def _():
        up_out[...] = jnp.zeros_like(up_out)

    @pl.when(last)
    def _():
        down_out[...] = jnp.zeros_like(down_out)

    def update(d, c, gradient):
        part = pl.ds(c * step, step)
        here = pl.ds(pl.multiple_of(along[d] * feats + c * step, step), step)
        gradient = gradient.astype(jnp.float32)
        new_first = beta_one * own_first[d, part] + (1.0 - beta_one) * gradient
        new_second = beta_two * own_second[d, part] + (1.0 - beta_two) * gradient * gradient
        first_hat = new_first * (1.0 / (1.0 - beta_one**ADAM_STEP))
        second_hat = new_second * (1.0 / (1.0 - beta_two**ADAM_STEP))
        held = own_weight[d, part].astype(jnp.float32)
        first_out[here] = new_first
        second_out[here] = new_second
        weight_out[here] = held - learn_rate * (
            first_hat / (jnp.sqrt(second_hat) + epsilon) + decay_rate * held
        )

    for c in range(CHUNKS):
        update(0, c, grads[0, pl.ds(c * step, step)])

    for c in range(CHUNKS):
        for copy, d in zip(grad_copies(c), others):
            copy.wait_recv()
            update(ways - d, c, arrived[ways - d, pl.ds(c * step, step)])

    for c in range(CHUNKS):
        @pl.when(jnp.logical_not(last))
        def _():
            down_copy(c).wait_recv()

        @pl.when(swaps)
        def _():
            up_copy(c).wait_recv()

    for c in range(CHUNKS):
        for copy in grad_copies(c) + weight_copies[c]:
            copy.wait_send()

        down_copy(c).wait_send()

        @pl.when(swaps)
        def _():
            up_copy(c).wait_send()

    for copy in [to_mirror, to_side, down_ahead, down_behind, up_behind, both_far, *row_copies]:
        copy.wait_send()


def relay(sections, ways, weight, first_moment, second_moment, down_rows, up_rows, down_grads, up_grads):
    feats, toks, cols = down_rows.shape[1], down_rows.shape[0], down_grads.shape[1]
    dma = pltpu.SemaphoreType.DMA
    state = pltpu.VMEM(weight.shape, jnp.float32)
    term = pltpu.VMEM((feats, toks), jnp.bfloat16)
    block = (ways, feats, cols)
    operands = [
        pltpu.with_memory_space_constraint(x, pltpu.HBM)
        for x in (weight, first_moment, second_moment, down_rows, up_rows, down_grads, up_grads)
    ]
    return pl.pallas_call(
        lambda *refs: relay_kernel(sections, ways, *refs),
        out_shape=(state, state, state, term, term),
        in_specs=[pl.BlockSpec(memory_space=pltpu.HBM)] * 7,
        out_specs=(pl.BlockSpec(memory_space=pltpu.VMEM),) * 5,
        scratch_shapes=[
            pltpu.VMEM(block, jnp.bfloat16),
            pltpu.VMEM(block, jnp.float32),
            pltpu.VMEM(block, jnp.float32),
            pltpu.VMEM((2 * toks, feats), jnp.bfloat16),
            pltpu.VMEM((ways, 2 * toks, cols), jnp.bfloat16),
            pltpu.VMEM(block, jnp.bfloat16),
            pltpu.VMEM(block, jnp.bfloat16),
            pltpu.VMEM(block, jnp.bfloat16),
            pltpu.VMEM((feats, toks), jnp.bfloat16),
            pltpu.VMEM((feats, toks), jnp.bfloat16),
            pltpu.VMEM((feats, toks), jnp.bfloat16),
            dma((2 + 3 * ways,)),
            dma((6,)),
            dma((6,)),
            dma((CHUNKS,)),
            dma((CHUNKS,)),
            dma((CHUNKS, ways)),
            dma((CHUNKS, ways)),
            dma((CHUNKS, ways)),
            dma((CHUNKS, ways)),
            dma((2, CHUNKS)),
            dma((2, CHUNKS)),
            dma((CHUNKS,)),
        ],
        compiler_params=pltpu.CompilerParams(
            collective_id=0, has_side_effects=True, vmem_limit_bytes=16 * 1024 * 1024
        ),
    )(*operands)


def leave_kernel(*refs):
    count = len(refs) // 2
    sems = refs[-1]
    copies = [
        pltpu.make_async_copy(refs[i], refs[count + i], sems.at[i]) for i in range(count)
    ]
    for copy in copies:
        copy.start()
    for copy in copies:
        copy.wait()


def leave(*arrays):
    return pl.pallas_call(
        leave_kernel,
        out_shape=tuple(jax.ShapeDtypeStruct(x.shape, x.dtype) for x in arrays),
        in_specs=[pl.BlockSpec(memory_space=pltpu.VMEM)] * len(arrays),
        out_specs=(pl.BlockSpec(memory_space=pl.ANY),) * len(arrays),
        scratch_shapes=[pltpu.SemaphoreType.DMA((len(arrays),))],
        compiler_params=pltpu.CompilerParams(vmem_limit_bytes=16 * 1024 * 1024),
    )(*(pltpu.with_memory_space_constraint(x, pltpu.VMEM) for x in arrays))


def local(
    key_weight, first_moment, second_moment, down_inputs, up_inputs, down_key_grads, up_key_grads
):
    arrays = relay(
        lax.axis_size("section"),
        lax.axis_size("tensor"),
        key_weight[0],
        first_moment[0],
        second_moment[0],
        down_inputs[0],
        up_inputs[0],
        down_key_grads[0],
        up_key_grads[0],
    )
    return tuple(x[None] for x in leave(*arrays))


def solution(mesh):
    in_specs = (
        P("section", None, "tensor"),
        P("section", None, "tensor"),
        P("section", None, "tensor"),
        P("section", None, "tensor"),
        P("section", None, "tensor"),
        P("section", None, "tensor"),
        P("section", None, "tensor"),
    )
    out_specs = (
        P("section", None, "tensor"),
        P("section", None, "tensor"),
        P("section", None, "tensor"),
        P("section", "tensor", None),
        P("section", "tensor", None),
    )
    return jax.shard_map(local, mesh=mesh, in_specs=in_specs, out_specs=out_specs, check_vma=False)
```

```python
import jax
import jax.numpy as jnp
from jax import lax
from jax.experimental import pallas as pl
from jax.experimental.pallas import tpu as pltpu
from jax.sharding import PartitionSpec as P

ADAM_STEP = 100


beta_one = 0.9
beta_two = 0.95
learn_rate = 0.00015
decay_rate = 0.1
epsilon = 1e-08

MESH = pl.DeviceIdType.MESH
CHUNKS = 4
EARLY = 2
RELAYED = 3


def relay_kernel(
    sections,
    ways,
    weight,
    first_moment,
    second_moment,
    down_rows,
    up_rows,
    down_grads,
    up_grads,
    weight_out,
    first_out,
    second_out,
    down_out,
    up_out,
    own_weight,
    own_first,
    own_second,
    tokens,
    keys,
    rows,
    grads,
    arrived,
    down_term,
    up_term,
    passing,
    ready,
    local_sem,
    key_send,
    key_recv,
    row_send,
    row_recv,
    weight_send,
    weight_recv,
    grad_send,
    grad_recv,
    term_send,
    term_recv,
    pass_recv,
):
    s = lax.axis_index("section")
    t = lax.axis_index("tensor")
    mirror = sections - 1 - s
    after = sections - s
    half = sections // 2
    toks, feats = down_rows.shape
    cols = down_grads.shape[1]
    step = feats // CHUNKS
    others = range(1, ways)
    back = ways - 1
    far = ways // 2
    along = [lax.rem(t + d, ways) for d in range(ways)]
    down_part, up_part = pl.ds(0, toks), pl.ds(toks, toks)

    def remote(src, dst, send, recv, where):
        return pltpu.make_async_remote_copy(
            src_ref=src, dst_ref=dst, send_sem=send, recv_sem=recv, device_id=where, device_id_type=MESH
        )

    barrier = pltpu.get_barrier_semaphore()

    def greet(where):
        pl.semaphore_signal(barrier, inc=1, device_id=where, device_id_type=MESH)

    late = t >= far
    side = lax.rem(t + jnp.where(s < half, back, 1), ways)
    peers = [(s, along[d]) for d in others] + [(mirror, side)]
    greet((mirror, t))
    for peer in peers:

        @pl.when(jnp.logical_not(jnp.logical_and(late, peer[1] < far)))
        def _():
            greet(peer)

    first, last, middle = s == 0, s == sections - 1, s == half
    joint = s == half - 1

    @pl.when(jnp.logical_not(jnp.logical_or(last, joint)))
    def _():
        greet((s + 1, t))

    @pl.when(joint)
    def _():
        greet((0, t))
        greet((half, t))

    @pl.when(first)
    def _():
        greet((half, t))

    swaps = jnp.logical_not(jnp.logical_or(first, middle))

    @pl.when(swaps)
    def _():
        greet((after, t))

    own = [
        pltpu.make_async_copy(down_grads, keys.at[0, down_part], local_sem.at[0]),
        pltpu.make_async_copy(down_rows, tokens.at[down_part], local_sem.at[1]),
    ]
    for d in range(ways):
        block = pl.ds(along[d] * feats, feats)
        own += [
            pltpu.make_async_copy(weight.at[block], own_weight.at[d], local_sem.at[2 + 3 * d]),
            pltpu.make_async_copy(first_moment.at[block], own_first.at[d], local_sem.at[3 + 3 * d]),
            pltpu.make_async_copy(second_moment.at[block], own_second.at[d], local_sem.at[4 + 3 * d]),
        ]
    for copy in own:
        copy.start()

    side_late = (side >= far).astype(jnp.int32)
    later = jnp.where(late, 0, ways - far + side_late)
    pl.semaphore_wait(barrier, ways + 2 + (swaps | middle).astype(jnp.int32) - later)

    for peer in peers:

        @pl.when(jnp.logical_and(late, peer[1] < far))
        def _():
            pl.semaphore_signal(ready, inc=1, device_id=peer, device_id_type=MESH)

    turn = jnp.where(s < half, 1, back)
    other = ways - turn
    ahead, behind = (s, lax.rem(t + turn, ways)), (s, lax.rem(t + other, ways))
    to_mirror = remote(up_grads, keys.at[0, up_part], key_send.at[0], key_recv.at[0], (mirror, t))
    to_side = remote(
        up_grads, keys.at[turn, up_part], key_send.at[1], key_recv.at[1], (mirror, lax.rem(t + other, ways))
    )
    down_ahead = remote(down_grads, keys.at[other, down_part], key_send.at[2], key_recv.at[2], ahead)
    down_behind = remote(down_grads, keys.at[turn, down_part], key_send.at[3], key_recv.at[3], behind)
    up_behind = remote(keys.at[0, up_part], keys.at[turn, up_part], key_send.at[4], key_recv.at[4], behind)
    both_far = remote(keys.at[other], keys.at[far], key_send.at[5], key_recv.at[5], ahead)
    row_copies = [
        remote(
            up_rows.at[:, pl.ds(c * step, step)],
            tokens.at[up_part, pl.ds(c * step, step)],
            row_send.at[c],
            row_recv.at[c],
            (mirror, t),
        )
        for c in range(CHUNKS)
    ]
    def weight_copy(c, d):
        there = lax.rem(t + d, ways)
        return remote(
            weight.at[pl.ds(there * feats + c * step, step)],
            rows.at[ways - d, pl.ds(c * step, step)],
            weight_send.at[c, d],
            weight_recv.at[c, ways - d],
            (s, there),
        )

    weight_copies = [[weight_copy(c, d) for d in others] for c in range(CHUNKS)]
    near = jnp.where(lax.rem(t, 2) == 0, 1, back)

    to_mirror.start()
    for copy in row_copies:
        copy.start()
    for c in range(EARLY):
        weight_copy(c, near).start()

    @pl.when(jnp.logical_not(late))
    def _():
        pl.semaphore_wait(ready, ways - far + side_late)

    for copy in (to_side, down_ahead, down_behind):
        copy.start()
    for c in range(EARLY):
        weight_copy(c, far).start()
        weight_copy(c, ways - near).start()
    to_mirror.wait_recv()
    up_behind.start()
    to_side.wait_recv()
    down_ahead.wait_recv()
    both_far.start()
    for copies in weight_copies[EARLY:]:
        for copy in copies:
            copy.start()
    for copy in own:
        copy.wait()
    for copy in (down_behind, up_behind, both_far):
        copy.wait_recv()

    def down_copy(c):
        part = pl.ds(c * step, step)
        return remote(
            down_term.at[part], down_out.at[part], term_send.at[0, c], term_recv.at[0, c], (s - 1, t)
        )

    def first_leg(c):
        part = pl.ds(c * step, step)
        return remote(down_term.at[part], passing.at[part], term_send.at[0, c], pass_recv.at[c], (0, t))

    def direct(c):
        part = pl.ds(c * step, step)
        return remote(
            down_term.at[part], down_out.at[part], term_send.at[0, c], term_recv.at[0, c], (half - 1, t)
        )

    def second_leg(c):
        part = pl.ds(c * step, step)
        return remote(
            passing.at[part], down_out.at[part], term_send.at[0, c], term_recv.at[0, c], (half - 1, t)
        )

    def up_copy(c):
        part = pl.ds(c * step, step)
        return remote(
            up_term.at[part], up_out.at[part], term_send.at[1, c], term_recv.at[1, c], (after, t)
        )

    sends_on = jnp.logical_not(jnp.logical_or(first, middle))

    def make_terms(c):
        part = pl.ds(c * step, step)
        for copy in weight_copies[c]:
            copy.wait_recv()
        all_keys = jnp.concatenate([keys[d] for d in range(ways)], axis=1)
        all_rows = jnp.concatenate(
            [own_weight[0, part]] + [rows[d, part] for d in others], axis=1
        )
        found = lax.dot_general(
            all_rows, all_keys, (((1,), (1,)), ((), ())), preferred_element_type=jnp.float32
        ).astype(jnp.bfloat16)
        down_term[part] = found[:, :toks]
        up_term[part] = found[:, toks:]

        @pl.when(sends_on)
        def _():
            up_copy(c).start()

        @pl.when(middle)
        def _():
            (first_leg(c) if c < RELAYED else direct(c)).start()
            up_out[part] = found[:, toks:]


    def grad_copies(c):
        part = pl.ds(c * step, step)
        return [
            remote(
                grads.at[d, part],
                arrived.at[ways - d, part],
                grad_send.at[c, d],
                grad_recv.at[c, ways - d],
                (s, along[d]),
            )
            for d in others
        ]

    def send_grads(c, low, high):
        part = pl.ds(c * step, step)
        for there in range(low, high):
            d = lax.rem(there + ways - t, ways)

            @pl.when(d != 0)
            def _():
                remote(
                    grads.at[d, part],
                    arrived.at[ways - d, part],
                    grad_send.at[c, d],
                    grad_recv.at[c, ways - d],
                    (s, there),
                ).start()

    def make_grads(c):
        part = pl.ds(c * step, step)
        row_copies[c].wait_recv()
        all_keys = jnp.concatenate([keys[d] for d in range(ways)], axis=1)
        found = lax.dot_general(
            tokens[:, part], all_keys, (((0,), (0,)), ((), ())), preferred_element_type=jnp.float32
        ).astype(jnp.bfloat16)
        for d in range(ways):
            grads[d, part] = found[:, d * cols : (d + 1) * cols]

    ends = jnp.logical_or(first, middle)
    early_rest = jnp.logical_and(t < far, jnp.logical_not(ends))
    late_rest = jnp.logical_and(t >= far, jnp.logical_not(ends))
    early_middle = jnp.logical_and(t < far, middle)
    late_middle = jnp.logical_and(t >= far, middle)

    @pl.when(early_rest)
    def _():
        make_terms(0)
        make_terms(1)
        make_grads(0)
        send_grads(0, 0, far)
        make_terms(2)
        make_grads(1)
        send_grads(1, 0, far)
        send_grads(0, far, ways)
        make_terms(3)
        make_grads(2)
        send_grads(2, 0, far)
        send_grads(1, far, ways)
        make_grads(3)
        send_grads(3, 0, far)
        send_grads(2, far, ways)
        send_grads(3, far, ways)

    @pl.when(late_rest)
    def _():
        make_grads(0)
        send_grads(0, 0, far)
        make_grads(1)
        send_grads(1, 0, far)
        make_grads(2)
        send_grads(2, 0, far)
        make_grads(3)
        send_grads(3, 0, far)
        make_terms(0)
        send_grads(0, far, ways)
        make_terms(1)
        send_grads(1, far, ways)
        make_terms(2)
        send_grads(2, far, ways)
        make_terms(3)
        send_grads(3, far, ways)

    @pl.when(early_middle)
    def _():
        make_grads(0)
        send_grads(0, 0, far)
        make_grads(1)
        send_grads(1, 0, far)
        make_grads(2)
        send_grads(2, 0, far)
        make_grads(3)
        send_grads(3, 0, far)
        make_terms(0)
        make_terms(1)
        make_terms(2)
        make_terms(3)
        send_grads(0, far, ways)
        send_grads(1, far, ways)
        send_grads(2, far, ways)
        send_grads(3, far, ways)

    @pl.when(late_middle)
    def _():
        make_terms(0)
        make_terms(1)
        make_terms(2)
        make_grads(0)
        send_grads(0, 0, far)
        make_grads(1)
        send_grads(1, 0, far)
        make_grads(2)
        send_grads(2, 0, far)
        make_grads(3)
        send_grads(3, 0, far)
        make_terms(3)
        send_grads(0, far, ways)
        send_grads(1, far, ways)
        send_grads(2, far, ways)
        send_grads(3, far, ways)

    @pl.when(first)
    def _():
        make_grads(0)
        send_grads(0, 0, far)
        make_grads(1)
        send_grads(1, 0, far)
        make_grads(2)
        send_grads(2, 0, far)
        make_grads(3)
        send_grads(3, 0, far)
        send_grads(0, far, ways)
        send_grads(1, far, ways)
        send_grads(2, far, ways)
        send_grads(3, far, ways)

    @pl.when(sends_on)
    def _():
        for c in range(CHUNKS):
            down_copy(c).start()

    @pl.when(first)
    def _():
        for c in range(RELAYED):
            first_leg(c).wait_recv()
            second_leg(c).start()
        for copies in weight_copies:
            for copy in copies:
                copy.wait_recv()

    @pl.when(first)
    def _():
        up_out[...] = jnp.zeros_like(up_out)

    @pl.when(last)
    def _():
        down_out[...] = jnp.zeros_like(down_out)

    def update(d, c, gradient):
        part = pl.ds(c * step, step)
        here = pl.ds(pl.multiple_of(along[d] * feats + c * step, step), step)
        gradient = gradient.astype(jnp.float32)
        new_first = beta_one * own_first[d, part] + (1.0 - beta_one) * gradient
        new_second = beta_two * own_second[d, part] + (1.0 - beta_two) * gradient * gradient
        first_hat = new_first * (1.0 / (1.0 - beta_one**ADAM_STEP))
        second_hat = new_second * (1.0 / (1.0 - beta_two**ADAM_STEP))
        held = own_weight[d, part].astype(jnp.float32)
        first_out[here] = new_first
        second_out[here] = new_second
        weight_out[here] = held - learn_rate * (
            first_hat / (jnp.sqrt(second_hat) + epsilon) + decay_rate * held
        )

    for c in range(CHUNKS):
        update(0, c, grads[0, pl.ds(c * step, step)])

    for c in range(CHUNKS):
        for copy, d in zip(grad_copies(c), others):
            copy.wait_recv()
            update(ways - d, c, arrived[ways - d, pl.ds(c * step, step)])

    for c in range(CHUNKS):
        @pl.when(jnp.logical_not(last))
        def _():
            down_copy(c).wait_recv()

        @pl.when(swaps)
        def _():
            up_copy(c).wait_recv()

    for c in range(CHUNKS):
        for copy in grad_copies(c) + weight_copies[c]:
            copy.wait_send()

        @pl.when(jnp.logical_or(jnp.logical_not(first), c < RELAYED))
        def _():
            down_copy(c).wait_send()

        @pl.when(swaps)
        def _():
            up_copy(c).wait_send()

    for copy in [to_mirror, to_side, down_ahead, down_behind, up_behind, both_far, *row_copies]:
        copy.wait_send()


def relay(sections, ways, weight, first_moment, second_moment, down_rows, up_rows, down_grads, up_grads):
    feats, toks, cols = down_rows.shape[1], down_rows.shape[0], down_grads.shape[1]
    dma = pltpu.SemaphoreType.DMA
    state = pltpu.VMEM(weight.shape, jnp.float32)
    term = pltpu.VMEM((feats, toks), jnp.bfloat16)
    block = (ways, feats, cols)
    operands = [
        pltpu.with_memory_space_constraint(x, pltpu.HBM)
        for x in (weight, first_moment, second_moment, down_rows, up_rows, down_grads, up_grads)
    ]
    return pl.pallas_call(
        lambda *refs: relay_kernel(sections, ways, *refs),
        out_shape=(state, state, state, term, term),
        in_specs=[pl.BlockSpec(memory_space=pltpu.HBM)] * 7,
        out_specs=(pl.BlockSpec(memory_space=pltpu.VMEM),) * 5,
        scratch_shapes=[
            pltpu.VMEM(block, jnp.bfloat16),
            pltpu.VMEM(block, jnp.float32),
            pltpu.VMEM(block, jnp.float32),
            pltpu.VMEM((2 * toks, feats), jnp.bfloat16),
            pltpu.VMEM((ways, 2 * toks, cols), jnp.bfloat16),
            pltpu.VMEM(block, jnp.bfloat16),
            pltpu.VMEM(block, jnp.bfloat16),
            pltpu.VMEM(block, jnp.bfloat16),
            pltpu.VMEM((feats, toks), jnp.bfloat16),
            pltpu.VMEM((feats, toks), jnp.bfloat16),
            pltpu.VMEM((feats, toks), jnp.bfloat16),
            pltpu.SemaphoreType.REGULAR,
            dma((2 + 3 * ways,)),
            dma((6,)),
            dma((6,)),
            dma((CHUNKS,)),
            dma((CHUNKS,)),
            dma((CHUNKS, ways)),
            dma((CHUNKS, ways)),
            dma((CHUNKS, ways)),
            dma((CHUNKS, ways)),
            dma((2, CHUNKS)),
            dma((2, CHUNKS)),
            dma((CHUNKS,)),
        ],
        compiler_params=pltpu.CompilerParams(
            collective_id=0, has_side_effects=True, vmem_limit_bytes=16 * 1024 * 1024
        ),
    )(*operands)


def leave_kernel(*refs):
    count = len(refs) // 2
    sems = refs[-1]
    copies = [
        pltpu.make_async_copy(refs[i], refs[count + i], sems.at[i]) for i in range(count)
    ]
    for copy in copies:
        copy.start()
    for copy in copies:
        copy.wait()


def leave(*arrays):
    return pl.pallas_call(
        leave_kernel,
        out_shape=tuple(jax.ShapeDtypeStruct(x.shape, x.dtype) for x in arrays),
        in_specs=[pl.BlockSpec(memory_space=pltpu.VMEM)] * len(arrays),
        out_specs=(pl.BlockSpec(memory_space=pl.ANY),) * len(arrays),
        scratch_shapes=[pltpu.SemaphoreType.DMA((len(arrays),))],
        compiler_params=pltpu.CompilerParams(vmem_limit_bytes=16 * 1024 * 1024),
    )(*(pltpu.with_memory_space_constraint(x, pltpu.VMEM) for x in arrays))


def local(
    key_weight, first_moment, second_moment, down_inputs, up_inputs, down_key_grads, up_key_grads
):
    arrays = relay(
        lax.axis_size("section"),
        lax.axis_size("tensor"),
        key_weight[0],
        first_moment[0],
        second_moment[0],
        down_inputs[0],
        up_inputs[0],
        down_key_grads[0],
        up_key_grads[0],
    )
    return tuple(x[None] for x in leave(*arrays))


def solution(mesh):
    in_specs = (
        P("section", None, "tensor"),
        P("section", None, "tensor"),
        P("section", None, "tensor"),
        P("section", None, "tensor"),
        P("section", None, "tensor"),
        P("section", None, "tensor"),
        P("section", None, "tensor"),
    )
    out_specs = (
        P("section", None, "tensor"),
        P("section", None, "tensor"),
        P("section", None, "tensor"),
        P("section", "tensor", None),
        P("section", "tensor", None),
    )
    return jax.shard_map(local, mesh=mesh, in_specs=in_specs, out_specs=out_specs, check_vma=False)
```

```python
import jax
import jax.numpy as jnp
from jax import lax
from jax.experimental import pallas as pl
from jax.experimental.pallas import tpu as pltpu
from jax.sharding import PartitionSpec as P

ADAM_STEP = 100


beta_one = 0.9
beta_two = 0.95
learn_rate = 0.00015
decay_rate = 0.1
epsilon = 1e-08

MESH = pl.DeviceIdType.MESH
CHUNKS = 4
EARLY = 2
RELAYED = 3


def relay_kernel(
    sections,
    ways,
    weight,
    first_moment,
    second_moment,
    down_rows,
    up_rows,
    down_grads,
    up_grads,
    weight_out,
    first_out,
    second_out,
    down_out,
    up_out,
    own_weight,
    own_first,
    own_second,
    tokens,
    keys,
    rows,
    grads,
    arrived,
    down_term,
    up_term,
    passing,
    ready,
    local_sem,
    key_send,
    key_recv,
    row_send,
    row_recv,
    weight_send,
    weight_recv,
    grad_send,
    grad_recv,
    term_send,
    term_recv,
    pass_recv,
):
    s = lax.axis_index("section")
    t = lax.axis_index("tensor")
    mirror = sections - 1 - s
    after = sections - s
    before = lax.rem(s - 1 + sections, sections)
    half = sections // 2
    toks, feats = down_rows.shape
    cols = down_grads.shape[1]
    step = feats // CHUNKS
    others = range(1, ways)
    back = ways - 1
    far = ways // 2
    along = [lax.rem(t + d, ways) for d in range(ways)]
    down_part, up_part = pl.ds(0, toks), pl.ds(toks, toks)

    def remote(src, dst, send, recv, where):
        return pltpu.make_async_remote_copy(
            src_ref=src, dst_ref=dst, send_sem=send, recv_sem=recv, device_id=where, device_id_type=MESH
        )

    barrier = pltpu.get_barrier_semaphore()

    def greet(where):
        pl.semaphore_signal(barrier, inc=1, device_id=where, device_id_type=MESH)

    late = t >= far
    side = lax.rem(t + jnp.where(s < half, back, 1), ways)
    peers = [(s, along[d]) for d in others] + [(mirror, side)]
    greet((mirror, t))
    for peer in peers:

        @pl.when(jnp.logical_not(jnp.logical_and(late, peer[1] < far)))
        def _():
            greet(peer)

    first, last, middle = s == 0, s == sections - 1, s == half
    joint = s == half - 1

    @pl.when(jnp.logical_not(jnp.logical_or(last, joint)))
    def _():
        greet((s + 1, t))

    @pl.when(joint)
    def _():
        greet((0, t))
        greet((half, t))

    @pl.when(first)
    def _():
        greet((half, t))

    swaps = jnp.logical_not(jnp.logical_or(first, middle))

    @pl.when(swaps)
    def _():
        greet((after, t))

    own = [
        pltpu.make_async_copy(down_grads, keys.at[0, down_part], local_sem.at[0]),
        pltpu.make_async_copy(down_rows, tokens.at[down_part], local_sem.at[1]),
    ]
    for d in range(ways):
        block = pl.ds(along[d] * feats, feats)
        own += [
            pltpu.make_async_copy(weight.at[block], own_weight.at[d], local_sem.at[2 + 3 * d]),
            pltpu.make_async_copy(first_moment.at[block], own_first.at[d], local_sem.at[3 + 3 * d]),
            pltpu.make_async_copy(second_moment.at[block], own_second.at[d], local_sem.at[4 + 3 * d]),
        ]
    for copy in own:
        copy.start()

    side_late = (side >= far).astype(jnp.int32)
    later = jnp.where(late, 0, ways - far + side_late)
    pl.semaphore_wait(barrier, ways + 2 + (swaps | middle).astype(jnp.int32) - later)

    for peer in peers:

        @pl.when(jnp.logical_and(late, peer[1] < far))
        def _():
            pl.semaphore_signal(ready, inc=1, device_id=peer, device_id_type=MESH)

    turn = jnp.where(s < half, 1, back)
    other = ways - turn
    ahead, behind = (s, lax.rem(t + turn, ways)), (s, lax.rem(t + other, ways))
    to_mirror = remote(up_grads, keys.at[0, up_part], key_send.at[0], key_recv.at[0], (mirror, t))
    to_side = remote(
        up_grads, keys.at[turn, up_part], key_send.at[1], key_recv.at[1], (mirror, lax.rem(t + other, ways))
    )
    down_ahead = remote(down_grads, keys.at[other, down_part], key_send.at[2], key_recv.at[2], ahead)
    down_behind = remote(down_grads, keys.at[turn, down_part], key_send.at[3], key_recv.at[3], behind)
    up_behind = remote(keys.at[0, up_part], keys.at[turn, up_part], key_send.at[4], key_recv.at[4], behind)
    both_far = remote(keys.at[other], keys.at[far], key_send.at[5], key_recv.at[5], ahead)
    row_copies = [
        remote(
            up_rows.at[:, pl.ds(c * step, step)],
            tokens.at[up_part, pl.ds(c * step, step)],
            row_send.at[c],
            row_recv.at[c],
            (mirror, t),
        )
        for c in range(CHUNKS)
    ]
    def weight_copy(c, d):
        there = lax.rem(t + d, ways)
        return remote(
            weight.at[pl.ds(there * feats + c * step, step)],
            rows.at[ways - d, pl.ds(c * step, step)],
            weight_send.at[c, d],
            weight_recv.at[c, ways - d],
            (s, there),
        )

    weight_copies = [[weight_copy(c, d) for d in others] for c in range(CHUNKS)]
    near = jnp.where(lax.rem(t, 2) == 0, 1, back)

    to_mirror.start()
    for copy in row_copies:
        copy.start()
    for c in range(EARLY):
        weight_copy(c, near).start()

    @pl.when(jnp.logical_not(late))
    def _():
        pl.semaphore_wait(ready, ways - far + side_late)

    for copy in (to_side, down_ahead, down_behind):
        copy.start()
    for c in range(EARLY):
        weight_copy(c, far).start()
        weight_copy(c, ways - near).start()
    to_mirror.wait_recv()
    up_behind.start()
    to_side.wait_recv()
    down_ahead.wait_recv()
    both_far.start()
    for copies in weight_copies[EARLY:]:
        for copy in copies:
            copy.start()
    for copy in own:
        copy.wait()
    for copy in (down_behind, up_behind, both_far):
        copy.wait_recv()

    def down_copy(c):
        part = pl.ds(c * step, step)
        return remote(
            down_term.at[part], down_out.at[part], term_send.at[0, c], term_recv.at[0, c], (before, t)
        )

    def first_leg(c):
        part = pl.ds(c * step, step)
        return remote(down_term.at[part], passing.at[part], term_send.at[0, c], pass_recv.at[c], (0, t))

    def direct(c):
        part = pl.ds(c * step, step)
        return remote(
            down_term.at[part], down_out.at[part], term_send.at[0, c], term_recv.at[0, c], (half - 1, t)
        )

    def second_leg(c):
        part = pl.ds(c * step, step)
        return remote(
            passing.at[part], down_out.at[part], term_send.at[0, c], term_recv.at[0, c], (half - 1, t)
        )

    def up_copy(c):
        part = pl.ds(c * step, step)
        return remote(
            up_term.at[part], up_out.at[part], term_send.at[1, c], term_recv.at[1, c], (after, t)
        )

    sends_on = jnp.logical_not(jnp.logical_or(first, middle))

    def make_terms(c):
        part = pl.ds(c * step, step)
        for copy in weight_copies[c]:
            copy.wait_recv()
        all_keys = jnp.concatenate([keys[d] for d in range(ways)], axis=1)
        all_rows = jnp.concatenate(
            [own_weight[0, part]] + [rows[d, part] for d in others], axis=1
        )
        found = lax.dot_general(
            all_rows, all_keys, (((1,), (1,)), ((), ())), preferred_element_type=jnp.float32
        ).astype(jnp.bfloat16)
        down_term[part] = found[:, :toks]
        up_term[part] = found[:, toks:]

        @pl.when(sends_on)
        def _():
            up_copy(c).start()

        @pl.when(middle)
        def _():
            (first_leg(c) if c < RELAYED else direct(c)).start()
            up_out[part] = found[:, toks:]


    def grad_copies(c):
        part = pl.ds(c * step, step)
        return [
            remote(
                grads.at[d, part],
                arrived.at[ways - d, part],
                grad_send.at[c, d],
                grad_recv.at[c, ways - d],
                (s, along[d]),
            )
            for d in others
        ]

    def send_grads(c, low, high):
        part = pl.ds(c * step, step)
        for there in range(low, high):
            d = lax.rem(there + ways - t, ways)

            @pl.when(d != 0)
            def _():
                remote(
                    grads.at[d, part],
                    arrived.at[ways - d, part],
                    grad_send.at[c, d],
                    grad_recv.at[c, ways - d],
                    (s, there),
                ).start()

    def make_grads(c):
        part = pl.ds(c * step, step)
        row_copies[c].wait_recv()
        all_keys = jnp.concatenate([keys[d] for d in range(ways)], axis=1)
        found = lax.dot_general(
            tokens[:, part], all_keys, (((0,), (0,)), ((), ())), preferred_element_type=jnp.float32
        ).astype(jnp.bfloat16)
        for d in range(ways):
            grads[d, part] = found[:, d * cols : (d + 1) * cols]

    ends = jnp.logical_or(first, middle)
    early_rest = jnp.logical_and(t < far, jnp.logical_not(ends))
    late_rest = jnp.logical_and(t >= far, jnp.logical_not(ends))
    early_middle = jnp.logical_and(t < far, middle)
    late_middle = jnp.logical_and(t >= far, middle)

    @pl.when(early_rest)
    def _():
        make_terms(0)
        make_terms(1)
        make_grads(0)
        send_grads(0, 0, far)
        make_terms(2)
        make_grads(1)
        send_grads(1, 0, far)
        send_grads(0, far, ways)
        make_terms(3)
        make_grads(2)
        send_grads(2, 0, far)
        send_grads(1, far, ways)
        make_grads(3)
        send_grads(3, 0, far)
        send_grads(2, far, ways)
        send_grads(3, far, ways)

    @pl.when(late_rest)
    def _():
        make_grads(0)
        send_grads(0, 0, far)
        make_grads(1)
        send_grads(1, 0, far)
        make_grads(2)
        send_grads(2, 0, far)
        make_grads(3)
        send_grads(3, 0, far)
        make_terms(0)
        send_grads(0, far, ways)
        make_terms(1)
        send_grads(1, far, ways)
        make_terms(2)
        send_grads(2, far, ways)
        make_terms(3)
        send_grads(3, far, ways)

    @pl.when(early_middle)
    def _():
        make_grads(0)
        send_grads(0, 0, far)
        make_grads(1)
        send_grads(1, 0, far)
        make_grads(2)
        send_grads(2, 0, far)
        make_grads(3)
        send_grads(3, 0, far)
        make_terms(0)
        make_terms(1)
        make_terms(2)
        make_terms(3)
        send_grads(0, far, ways)
        send_grads(1, far, ways)
        send_grads(2, far, ways)
        send_grads(3, far, ways)

    @pl.when(late_middle)
    def _():
        make_terms(0)
        make_terms(1)
        make_terms(2)
        make_grads(0)
        send_grads(0, 0, far)
        make_grads(1)
        send_grads(1, 0, far)
        make_grads(2)
        send_grads(2, 0, far)
        make_grads(3)
        send_grads(3, 0, far)
        make_terms(3)
        send_grads(0, far, ways)
        send_grads(1, far, ways)
        send_grads(2, far, ways)
        send_grads(3, far, ways)

    @pl.when(first)
    def _():
        make_grads(0)
        send_grads(0, 0, far)
        make_grads(1)
        send_grads(1, 0, far)
        make_grads(2)
        send_grads(2, 0, far)
        make_grads(3)
        send_grads(3, 0, far)
        send_grads(0, far, ways)
        send_grads(1, far, ways)
        send_grads(2, far, ways)
        send_grads(3, far, ways)

    @pl.when(sends_on)
    def _():
        for c in range(CHUNKS):
            down_copy(c).start()

    @pl.when(first)
    def _():
        for c in range(RELAYED):
            first_leg(c).wait_recv()
            second_leg(c).start()
        for copies in weight_copies:
            for copy in copies:
                copy.wait_recv()

    @pl.when(first)
    def _():
        up_out[...] = jnp.zeros_like(up_out)

    @pl.when(last)
    def _():
        down_out[...] = jnp.zeros_like(down_out)

    def update(d, c, gradient):
        part = pl.ds(c * step, step)
        here = pl.ds(pl.multiple_of(along[d] * feats + c * step, step), step)
        gradient = gradient.astype(jnp.float32)
        new_first = beta_one * own_first[d, part] + (1.0 - beta_one) * gradient
        new_second = beta_two * own_second[d, part] + (1.0 - beta_two) * gradient * gradient
        first_hat = new_first * (1.0 / (1.0 - beta_one**ADAM_STEP))
        second_hat = new_second * (1.0 / (1.0 - beta_two**ADAM_STEP))
        held = own_weight[d, part].astype(jnp.float32)
        first_out[here] = new_first
        second_out[here] = new_second
        weight_out[here] = held - learn_rate * (
            first_hat / (jnp.sqrt(second_hat) + epsilon) + decay_rate * held
        )

    for c in range(CHUNKS):
        update(0, c, grads[0, pl.ds(c * step, step)])

    for c in range(CHUNKS):
        for copy, d in zip(grad_copies(c), others):
            copy.wait_recv()
            update(ways - d, c, arrived[ways - d, pl.ds(c * step, step)])

    for c in range(CHUNKS):
        @pl.when(jnp.logical_not(last))
        def _():
            down_copy(c).wait_recv()

        @pl.when(swaps)
        def _():
            up_copy(c).wait_recv()

    for c in range(CHUNKS):
        for copy in grad_copies(c) + weight_copies[c]:
            copy.wait_send()

        @pl.when(jnp.logical_or(jnp.logical_not(first), c < RELAYED))
        def _():
            down_copy(c).wait_send()

        @pl.when(swaps)
        def _():
            up_copy(c).wait_send()

    for copy in [to_mirror, to_side, down_ahead, down_behind, up_behind, both_far, *row_copies]:
        copy.wait_send()


def relay(sections, ways, weight, first_moment, second_moment, down_rows, up_rows, down_grads, up_grads):
    feats, toks, cols = down_rows.shape[1], down_rows.shape[0], down_grads.shape[1]
    dma = pltpu.SemaphoreType.DMA
    state = pltpu.VMEM(weight.shape, jnp.float32)
    term = pltpu.VMEM((feats, toks), jnp.bfloat16)
    block = (ways, feats, cols)
    operands = [
        pltpu.with_memory_space_constraint(x, pltpu.HBM)
        for x in (weight, first_moment, second_moment, down_rows, up_rows, down_grads, up_grads)
    ]
    return pl.pallas_call(
        lambda *refs: relay_kernel(sections, ways, *refs),
        out_shape=(state, state, state, term, term),
        in_specs=[pl.BlockSpec(memory_space=pltpu.HBM)] * 7,
        out_specs=(pl.BlockSpec(memory_space=pltpu.VMEM),) * 5,
        scratch_shapes=[
            pltpu.VMEM(block, jnp.bfloat16),
            pltpu.VMEM(block, jnp.float32),
            pltpu.VMEM(block, jnp.float32),
            pltpu.VMEM((2 * toks, feats), jnp.bfloat16),
            pltpu.VMEM((ways, 2 * toks, cols), jnp.bfloat16),
            pltpu.VMEM(block, jnp.bfloat16),
            pltpu.VMEM(block, jnp.bfloat16),
            pltpu.VMEM(block, jnp.bfloat16),
            pltpu.VMEM((feats, toks), jnp.bfloat16),
            pltpu.VMEM((feats, toks), jnp.bfloat16),
            pltpu.VMEM((feats, toks), jnp.bfloat16),
            pltpu.SemaphoreType.REGULAR,
            dma((2 + 3 * ways,)),
            dma((6,)),
            dma((6,)),
            dma((CHUNKS,)),
            dma((CHUNKS,)),
            dma((CHUNKS, ways)),
            dma((CHUNKS, ways)),
            dma((CHUNKS, ways)),
            dma((CHUNKS, ways)),
            dma((2, CHUNKS)),
            dma((2, CHUNKS)),
            dma((CHUNKS,)),
        ],
        compiler_params=pltpu.CompilerParams(
            collective_id=0, has_side_effects=True, vmem_limit_bytes=16 * 1024 * 1024
        ),
    )(*operands)


def leave_kernel(*refs):
    count = len(refs) // 2
    sems = refs[-1]
    copies = [
        pltpu.make_async_copy(refs[i], refs[count + i], sems.at[i]) for i in range(count)
    ]
    for copy in copies:
        copy.start()
    for copy in copies:
        copy.wait()


def leave(*arrays):
    return pl.pallas_call(
        leave_kernel,
        out_shape=tuple(jax.ShapeDtypeStruct(x.shape, x.dtype) for x in arrays),
        in_specs=[pl.BlockSpec(memory_space=pltpu.VMEM)] * len(arrays),
        out_specs=(pl.BlockSpec(memory_space=pl.ANY),) * len(arrays),
        scratch_shapes=[pltpu.SemaphoreType.DMA((len(arrays),))],
        compiler_params=pltpu.CompilerParams(vmem_limit_bytes=16 * 1024 * 1024),
    )(*(pltpu.with_memory_space_constraint(x, pltpu.VMEM) for x in arrays))


def local(
    key_weight, first_moment, second_moment, down_inputs, up_inputs, down_key_grads, up_key_grads
):
    arrays = relay(
        lax.axis_size("section"),
        lax.axis_size("tensor"),
        key_weight[0],
        first_moment[0],
        second_moment[0],
        down_inputs[0],
        up_inputs[0],
        down_key_grads[0],
        up_key_grads[0],
    )
    return tuple(x[None] for x in leave(*arrays))


def solution(mesh):
    in_specs = (
        P("section", None, "tensor"),
        P("section", None, "tensor"),
        P("section", None, "tensor"),
        P("section", None, "tensor"),
        P("section", None, "tensor"),
        P("section", None, "tensor"),
        P("section", None, "tensor"),
    )
    out_specs = (
        P("section", None, "tensor"),
        P("section", None, "tensor"),
        P("section", None, "tensor"),
        P("section", "tensor", None),
        P("section", "tensor", None),
    )
    return jax.shard_map(local, mesh=mesh, in_specs=in_specs, out_specs=out_specs, check_vma=False)
```
